32 devices in a mesh: seq: 8 (over y, x, core), tensor: 4 (over z).
Axes of the slice: x: 2, y: 2, z: 4, core: 2. Of those that a mesh axis runs over, the one named last changes fastest.
Arguments:
- tokens: bfloat16 [1024, 4096], P('seq'), may hold values from -8 to 8
- segment_ids: int32 [1024], replicated, may hold values from -1 to 14, as said below
- routes: int32 [1024, 2], P('seq'), may hold values from 0 to 7, all different within a row; in each aligned block of 128 rows (0 to 127, 128 to 255, ...) at most 64 rows name the same one
- owners: int32 [15], replicated, may hold values from 0 to 7
- gain_attn: float32 [4096], replicated, may hold values from 0.5 to 1.5
- w_query: bfloat16 [4096, 4096], P(None, 'tensor'), may hold values from -1 to 1
- w_kv: bfloat16 [4096, 2048], P(None, 'tensor'), may hold values from -1 to 1
- w_out: bfloat16 [4096, 4096], P('tensor'), may hold values from -0.09375 to 0.09375
- gain_moe: float32 [4096], replicated, may hold values from 0.5 to 1.5
- w_router: float32 [4096, 8], replicated, may hold values from -0.09375 to 0.09375
- w_gate: bfloat16 [4096, 65536], P(None, ('seq', 'tensor')), may hold values from -0.09375 to 0.09375
- w_up: bfloat16 [4096, 65536], P(None, ('seq', 'tensor')), may hold values from -0.09375 to 0.09375
- w_down: bfloat16 [65536, 4096], P(('seq', 'tensor')), may hold values from -0.0625 to 0.0625
Outputs:
- layer_out: bfloat16 [1024, 4096], P('seq', 'tensor')
- kv_cache: bfloat16 [8192, 2048], P('seq', 'tensor')
The draws below stay inside these ranges and needn't reach their ends.
Inputs may be any that keep to these rules, and one draw needn't show every extreme that they name: `segment_ids`: tokens 0 to 575 form segment 0; segments 1 to 14 follow in order, each of 8 to 31 tokens; all later tokens are -1. `routes`: in each aligned block of 128 rows no expert is named by more than 64 rows; the two experts of a row differ.
All inputs are finite; a program needn't handle non-finite values.
Results may differ from the reference program's by a relative error of at most 0.014.
Values may be sent and summed in bfloat16 or wider, within the bound.
A program may use at most 128 MiB of HBM per device.

```python
import math
import jax
import jax.numpy as jnp
import numpy as np
from jax import lax

D = 4096
HEADS = 32
KV_HEADS = 8
HEAD_DIM = 128
EXPERTS = 8
TOPK = 2
FF = 8192
NSHORT = 14
TOK_DEV = 128
TOKENS = 1024
LONG = 576
MOST = 64
N_SEQ = 8
N_TENSOR = 4


def draw_segment_ids(key, part):
    lengths = jax.random.randint(key, (NSHORT,), 8, 32, dtype=jnp.int32)
    ends = LONG + jnp.cumsum(lengths)
    index = jnp.arange(TOKENS, dtype=jnp.int32)
    later = 1 + jnp.sum((index[:, None] >= ends[None, :]).astype(jnp.int32), axis=1)
    labels = jnp.where(index < LONG, 0, later)
    return jnp.where(labels > NSHORT, -1, labels).astype(jnp.int32)


def draw_tokens(key, part):
    noise = jnp.clip(jax.random.normal(jax.random.fold_in(key, 10), (TOKENS, D), jnp.float32), -6.0, 6.0)
    return noise.astype(jnp.bfloat16)


def draw_w_query(key, part):
    columns = HEADS * HEAD_DIM
    bound = 6.0 / math.sqrt(D)
    base = jax.random.normal(jax.random.fold_in(key, 21), (D, columns), jnp.float32) / math.sqrt(D)
    return jnp.clip(base, -bound, bound).astype(jnp.bfloat16)


def draw_w_kv(key, part):
    columns = 2 * KV_HEADS * HEAD_DIM
    bound = 6.0 / math.sqrt(D)
    base = jax.random.normal(jax.random.fold_in(key, 22), (D, columns), jnp.float32) / math.sqrt(D)
    return jnp.clip(base, -bound, bound).astype(jnp.bfloat16)


def plant(values, rng, least, top_value):
    dims = values.shape
    place = [jax.random.randint(jax.random.fold_in(rng, axis), (), 0, dims[axis]) for axis in range(len(dims))]
    values = values.at[tuple(place)].set(least)
    longest = dims.index(max(dims))
    place[longest] = (place[longest] + 1) % dims[longest]
    return values.at[tuple(place)].set(top_value)


def steps_of(rng, dims, split, low, high):
    loudness = 1.0
    for dim, blocks in split:
        draws = jax.random.uniform(jax.random.fold_in(jax.random.fold_in(rng, 6), dim), (blocks,), jnp.float32, low / len(split), high / len(split))
        loudness = loudness * jnp.repeat(jnp.exp(draws), dims[dim] // blocks).reshape((-1,) + (1,) * (len(dims) - 1 - dim))
    return loudness


def shared_out(key, own, number, rows, count, top, limit, lean):
    order = jax.random.permutation(key, count)
    crowded, common = load_shares(count, rows * top, limit, lean, True), load_shares(count, rows * top, limit, lean, False)
    places = jnp.arange(count)

    def named(tallies, offset_by):
        used = int((tallies > 0).sum())
        fixed = max(1, used // 4)
        moved = fixed + (places - fixed + offset_by * (used - fixed)) % max(1, count - fixed)
        return jnp.zeros((count,), jnp.int32).at[order[jnp.where(places < fixed, places, moved)]].set(jnp.asarray(tallies, jnp.int32))

    tallies = jnp.where(number % 4 == 0, named(crowded, number // 4), named(common, number - number // 4 - 1))
    mixed = jax.random.permutation(jax.random.fold_in(own, 3), count)
    source_of, receiver = mixed[0:count // 2 * 2:2], mixed[1:count // 2 * 2:2]
    margin = jnp.minimum(tallies[source_of] - 1, limit - tallies[receiver]) // 2
    margin = jnp.where((source_of == order[0]) | (receiver == order[0]) | (tallies[receiver] == 0), 0, jnp.maximum(margin, 0))
    moved = jax.random.randint(jax.random.fold_in(own, 4), (count // 2,), 0, 1 << 20) % (margin + 1)
    tallies = tallies.at[source_of].add(-moved).at[receiver].add(moved)
    items = jnp.searchsorted(jnp.cumsum(tallies), jnp.arange(rows * top), side="right").astype(jnp.int32)
    grid = items.reshape(top, rows).T
    grid = grid[jax.random.permutation(jax.random.fold_in(own, 1), rows)]
    offset_by = jax.random.randint(jax.random.fold_in(own, 2), (rows, 1), 0, top)
    return jnp.take_along_axis(grid, (jnp.arange(top)[None, :] + offset_by) % top, axis=1)


def load_shares(count, total, most, lean, full):
    portions = [(1 << 20) // math.isqrt(standing ** lean) + 1 for standing in range(1, count + 1)]
    largest = most if full else min(most, max(-(-total // count), total * portions[0] // sum(portions)))
    least = 1 if total - largest >= count - 1 else 0
    given, rest = [largest] + [least] * (count - 1), total - largest - least * (count - 1)
    while rest > 0:
        movable = [i for i in range(1, count) if given[i] < largest] or [i for i in range(1, count) if given[i] < most]
        mass, budget = sum([portions[i] for i in movable]), rest
        for i in movable:
            more = min(most - given[i], max(1, budget * portions[i] // mass), rest)
            given[i] = given[i] + more
            rest = rest - more
    return np.array(given)


def centred(own_key, extent, deviation, most, cuts=(), kind=jnp.bfloat16):
    values = jax.random.normal(own_key, extent, jnp.float32) * deviation
    if len(cuts) > 0:
        values = steps_of(own_key, extent, cuts, -0.22, 0.18) * values
    return jnp.clip(values, min=-most, max=most).astype(kind)


def setup_inputs(seed: int = 0) -> dict:
    splits = jax.random.split(jax.random.key(seed), 14)
    tokens = draw_tokens(jax.random.fold_in(splits[13], 71), 0)
    segment_ids = draw_segment_ids(jax.random.fold_in(splits[13], 71), 0)
    routes_keys = jax.random.split(jax.random.fold_in(splits[2], 1), TOKENS // TOK_DEV)
    routes_turns = jax.random.permutation(jax.random.fold_in(splits[2], 3), TOKENS // TOK_DEV)
    routes = jax.vmap(lambda own, number: shared_out(jax.random.fold_in(splits[2], 2), own, number, TOK_DEV, EXPERTS, TOPK, MOST, 2))(routes_keys, routes_turns).reshape((TOKENS, TOPK))
    owners = plant(jax.random.randint(splits[3], (NSHORT + 1,), 0, N_SEQ), jax.random.fold_in(splits[3], 1), 0, N_SEQ - 1).astype(jnp.int32)
    gain_attn = jnp.clip(1.0 + 0.1 * jax.random.normal(splits[4], (D,), jnp.float32), 0.5, 1.5)
    w_query = draw_w_query(jax.random.fold_in(splits[13], 71), 0)
    w_kv = draw_w_kv(jax.random.fold_in(splits[13], 71), 0)
    w_out = centred(splits[7], (HEADS * HEAD_DIM, D), (HEADS * HEAD_DIM) ** -0.5, 0.09375, ((0, 4),))
    gain_moe = jnp.clip(1.0 + 0.1 * jax.random.normal(splits[8], (D,), jnp.float32), 0.5, 1.5)
    w_router = centred(splits[9], (D, EXPERTS), D ** -0.5, 0.09375, (), jnp.float32)
    w_gate = centred(splits[10], (D, EXPERTS * FF), D ** -0.5, 0.09375, ((1, 32),))
    w_up = centred(splits[11], (D, EXPERTS * FF), D ** -0.5, 0.09375, ((1, 32),))
    w_down = centred(splits[12], (EXPERTS * FF, D), FF ** -0.5, 0.0625, ((0, 32),))
    return {"tokens": tokens, "segment_ids": segment_ids, "routes": routes, "owners": owners, "gain_attn": gain_attn, "w_query": w_query, "w_kv": w_kv, "w_out": w_out, "gain_moe": gain_moe, "w_router": w_router, "w_gate": w_gate, "w_up": w_up, "w_down": w_down}


EPS = 1e-05
THETA = 1000000.0
FLOOR = -1e+30

def settle(value):
    return lax.optimization_barrier(value.astype(jnp.bfloat16)).astype(jnp.float32)

def rms_norm(rows, gain):
    values = rows.astype(jnp.float32)
    scale = lax.rsqrt(lax.optimization_barrier(jnp.mean(values * values, axis=-1, keepdims=True)) + EPS)
    return (values * scale * gain).astype(jnp.bfloat16)

def rotate(values, position):
    half = values.shape[-1] // 2
    freqs = THETA ** (-(jnp.arange(half, dtype=jnp.float32) * 2.0) / values.shape[-1])
    angles = position.astype(jnp.float32)[:, None] * freqs[None, :]
    cosine = jnp.cos(angles)[:, None, :]
    sine = jnp.sin(angles)[:, None, :]
    first = values[..., :half]
    second = values[..., half:]
    return jnp.concatenate([first * cosine - second * sine, second * cosine + first * sine], axis=-1)

def segment_layout(segment_ids, owners):
    short_count = owners.shape[0] - 1
    labels = jnp.where(segment_ids < 0, short_count + 1, segment_ids).astype(jnp.int32)
    onehot = labels[:, None] == jnp.arange(short_count + 2, dtype=jnp.int32)[None, :]
    counts = lax.optimization_barrier(jnp.sum(onehot.astype(jnp.int32), axis=0)).astype(jnp.int32)
    starts = (jnp.cumsum(counts) - counts).astype(jnp.int32)
    seg_start = lax.optimization_barrier(jnp.sum(jnp.where(onehot, starts[None, :], 0), axis=1)).astype(jnp.int32)
    owner_ext = jnp.concatenate([owners.astype(jnp.int32), jnp.full((1,), -1, jnp.int32)])
    owner_tok = lax.optimization_barrier(jnp.sum(jnp.where(onehot, owner_ext[None, :], 0), axis=1)).astype(jnp.int32)
    return (seg_start, owner_tok)

def owner_slots(owner_tok, owner_count):
    hits = (owner_tok[:, None] == jnp.arange(owner_count, dtype=jnp.int32)[None, :]).astype(jnp.int32)
    before = jnp.cumsum(hits, axis=0) - hits
    return lax.optimization_barrier(jnp.sum(before * hits, axis=1)).astype(jnp.int32)

def reference(tokens, segment_ids, routes, owners, gain_attn, w_query, w_kv, w_out, gain_moe, w_router, w_gate, w_up, w_down):
    seg_start, owner_tok = segment_layout(segment_ids, owners)
    index = jnp.arange(TOKENS, dtype=jnp.int32)
    position = index - seg_start
    normed = rms_norm(tokens, gain_attn)
    queries = jnp.dot(normed, w_query, preferred_element_type=jnp.float32).reshape(TOKENS, HEADS, HEAD_DIM)
    queries = rotate(queries, position).astype(jnp.bfloat16)
    pairs = jnp.dot(normed, w_kv, preferred_element_type=jnp.float32).reshape(TOKENS, KV_HEADS, 2, HEAD_DIM)
    keys = rotate(pairs[:, :, 0], position).astype(jnp.bfloat16)
    values = pairs[:, :, 1].astype(jnp.bfloat16)
    group = HEADS // KV_HEADS
    grouped = queries.reshape(TOKENS, KV_HEADS, group, HEAD_DIM)
    allowed = (index[None, :] <= index[:, None]) & (index[None, :] >= seg_start[:, None])
    scale = HEAD_DIM ** (-0.5)

    def one_head(operands):
        query_head, key_head, value_head = operands
        scores = jnp.einsum('qgd,nd->gqn', query_head.astype(jnp.float32), key_head.astype(jnp.float32)) * scale
        scores = jnp.where(allowed[None], scores, FLOOR)
        top = lax.optimization_barrier(jnp.max(scores, axis=-1, keepdims=True))
        weights = jnp.where(allowed[None], jnp.exp(scores - top), 0.0)
        total = lax.optimization_barrier(jnp.sum(weights, axis=-1))
        mixed = jnp.einsum('gqn,nd->gqd', settle(weights), value_head.astype(jnp.float32))
        return mixed / total[..., None]
    heads_out = lax.map(one_head, (grouped.transpose(1, 0, 2, 3), keys.transpose(1, 0, 2), values.transpose(1, 0, 2)))
    attended = heads_out.transpose(2, 0, 1, 3).reshape(TOKENS, HEADS * HEAD_DIM).astype(jnp.bfloat16)
    attn_out = jnp.dot(attended, w_out, preferred_element_type=jnp.float32)
    residual = (tokens.astype(jnp.float32) + attn_out).astype(jnp.bfloat16)
    moe_in = rms_norm(residual, gain_moe)
    logits = jnp.dot(moe_in.astype(jnp.float32), w_router, preferred_element_type=jnp.float32)
    expert_ids = jnp.arange(EXPERTS, dtype=jnp.int32)
    picked = routes[:, :, None] == expert_ids[None, None, :]
    chosen = lax.optimization_barrier(jnp.sum(jnp.where(picked, logits[:, None, :], 0.0), axis=2))
    gates = jax.nn.softmax(chosen, axis=1)
    holders = N_SEQ // EXPERTS
    block = FF // (holders * N_TENSOR)
    bound = N_SEQ * MOST
    padded = jnp.concatenate([moe_in, jnp.zeros((1, D), jnp.bfloat16)], axis=0)

    def add_expert(expert, mixture):
        wg = lax.dynamic_slice_in_dim(w_gate, expert * FF, FF, 1)
        wu = lax.dynamic_slice_in_dim(w_up, expert * FF, FF, 1)
        wd = lax.dynamic_slice_in_dim(w_down, expert * FF, FF, 0)
        hit = jnp.any(routes == expert, axis=1)
        chosen_rows = jnp.nonzero(hit, size=bound, fill_value=TOKENS)[0].astype(jnp.int32)
        rows_in = padded[chosen_rows]
        active = (jax.nn.silu(jnp.dot(rows_in, wg, preferred_element_type=jnp.float32)) * jnp.dot(rows_in, wu, preferred_element_type=jnp.float32)).astype(jnp.bfloat16)
        result = jnp.zeros((bound, D), jnp.float32)
        for holder in range(holders):
            group_sum = jnp.zeros((bound, D), jnp.float32)
            for member in range(N_TENSOR):
                low = (holder * N_TENSOR + member) * block
                group_sum = group_sum + settle(jnp.dot(active[:, low:low + block], wd[low:low + block], preferred_element_type=jnp.float32))
            result = result + settle(group_sum)
        weight = lax.optimization_barrier(jnp.sum(jnp.where(routes == expert, gates, 0.0), axis=1))
        spread = jnp.zeros((TOKENS + 1, D), jnp.float32).at[chosen_rows].set(result)[:TOKENS]
        return mixture + weight[:, None] * spread
    mixture = lax.fori_loop(0, EXPERTS, add_expert, jnp.zeros((TOKENS, D), jnp.float32))
    layer_out = (residual.astype(jnp.float32) + mixture).astype(jnp.bfloat16)
    kv_rows = jnp.stack([keys, values], axis=2).reshape(TOKENS, 2 * KV_HEADS * HEAD_DIM)
    slots = owner_slots(owner_tok, N_SEQ)
    target = jnp.where(owner_tok >= 0, owner_tok * TOKENS + slots, N_SEQ * TOKENS).astype(jnp.int32)
    kv_cache = jnp.zeros((N_SEQ * TOKENS + 1, 2 * KV_HEADS * HEAD_DIM), jnp.bfloat16).at[target].set(kv_rows)[:N_SEQ * TOKENS]
    return (layer_out, kv_cache)
```

```python
import jax
import jax.numpy as jnp
from jax import lax
from jax.sharding import PartitionSpec as P

HEADS = 32
KV_HEADS = 8
HEAD_DIM = 128
EXPERTS = 8


EPS = 1e-05
THETA = 1000000.0
FLOOR = -1e30


def rms_norm(rows, gain):
    values = rows.astype(jnp.float32)
    scale = lax.rsqrt(jnp.mean(values * values, axis=-1, keepdims=True) + EPS)
    return (values * scale * gain).astype(jnp.bfloat16)


def rotate(values, position):
    half = values.shape[-1] // 2
    freqs = THETA ** (-(jnp.arange(half, dtype=jnp.float32) * 2.0) / values.shape[-1])
    angles = position.astype(jnp.float32)[:, None] * freqs[None, :]
    cosine = jnp.cos(angles)[:, None, :]
    sine = jnp.sin(angles)[:, None, :]
    first = values[..., :half]
    second = values[..., half:]
    return jnp.concatenate(
        [first * cosine - second * sine, second * cosine + first * sine], axis=-1
    )


def segment_layout(segment_ids, owners, token_index):
    short_count = owners.shape[0] - 1
    labels = jnp.where(segment_ids < 0, short_count + 1, segment_ids)
    mine = jnp.sum(
        jnp.where(
            jnp.arange(segment_ids.shape[0], dtype=jnp.int32)[None, :] == token_index[:, None],
            labels[None, :],
            0,
        ),
        axis=1,
    )
    seg_start = jnp.sum((labels[None, :] < mine[:, None]).astype(jnp.int32), axis=1)
    owner_ext = jnp.concatenate([owners, jnp.full((1,), -1, jnp.int32)])
    onehot = labels[:, None] == jnp.arange(short_count + 2, dtype=jnp.int32)[None, :]
    owner_all = jnp.sum(jnp.where(onehot, owner_ext[None, :], 0), axis=1)
    return (seg_start, owner_all)


def cache_places(owner_all, owner):
    total = owner_all.shape[0]
    index = jnp.arange(total, dtype=jnp.int32)
    mine = owner_all == owner
    slots = jnp.sum(((index[None, :] < index[:, None]) & mine[None, :]).astype(jnp.int32), axis=1)
    slots = jnp.where(mine, slots, total)
    return (index[:, None] == slots[None, :]).astype(jnp.bfloat16)


def local(
    tokens,
    segment_ids,
    routes,
    owners,
    gain_attn,
    w_query,
    w_kv,
    w_out,
    gain_moe,
    w_router,
    w_gate,
    w_up,
    w_down,
):
    seq_count = lax.axis_size("seq")
    ten_count = lax.axis_size("tensor")
    seq_rank = lax.axis_index("seq")
    ten_rank = lax.axis_index("tensor")
    rows, width = tokens.shape
    kv_local = w_kv.shape[1] // (2 * HEAD_DIM)
    kv_width = 2 * kv_local * HEAD_DIM
    group = HEADS // KV_HEADS
    first = seq_rank * rows
    token_index = first + jnp.arange(rows, dtype=jnp.int32)
    seg_start, owner_all = segment_layout(segment_ids, owners, token_index)
    position = token_index - seg_start
    normed = rms_norm(tokens, gain_attn)
    queries = jnp.dot(normed, w_query, preferred_element_type=jnp.float32).reshape(
        rows, kv_local * group, HEAD_DIM
    )
    queries = rotate(queries, position).astype(jnp.bfloat16)
    pairs = jnp.dot(normed, w_kv, preferred_element_type=jnp.float32).reshape(
        rows, kv_local, 2, HEAD_DIM
    )
    keys = rotate(pairs[:, :, 0], position).astype(jnp.bfloat16)
    values = pairs[:, :, 1].astype(jnp.bfloat16)
    grouped = queries.reshape(rows, kv_local, group, HEAD_DIM)
    scale = HEAD_DIM ** (-0.5)
    kv_rows = jnp.stack([keys, values], axis=2).reshape(rows, kv_width)
    piece = lax.all_gather(kv_rows, "seq", axis=0, tiled=True)
    kv_cache = jnp.dot(
        cache_places(owner_all, seq_rank), piece, preferred_element_type=jnp.float32
    ).astype(jnp.bfloat16)
    running = jnp.full((kv_local, group, rows), FLOOR, jnp.float32)
    count = piece.shape[0]
    pieces = piece.reshape(count, kv_local, 2, HEAD_DIM)
    key_piece = pieces[:, :, 0]
    value_piece = pieces[:, :, 1]
    key_index = jnp.arange(count, dtype=jnp.int32)
    allowed = (key_index[None, :] <= token_index[:, None]) & (
        key_index[None, :] >= seg_start[:, None]
    )
    scores = (
        jnp.einsum("qkgd,nkd->kgqn", grouped, key_piece, preferred_element_type=jnp.float32) * scale
    )
    scores = jnp.where(allowed[None, None], scores, FLOOR)
    new_top = jnp.maximum(running, jnp.max(scores, axis=-1))
    weights = jnp.where(allowed[None, None], jnp.exp(scores - new_top[..., None]), 0.0)
    mass = jnp.sum(weights, axis=-1)
    accum = jnp.einsum(
        "kgqn,nkd->kgqd",
        weights.astype(jnp.bfloat16),
        value_piece,
        preferred_element_type=jnp.float32,
    )
    running, mass, accum = (new_top, mass, accum)
    attended = (
        (accum / mass[..., None])
        .transpose(2, 0, 1, 3)
        .reshape(rows, kv_local * group * HEAD_DIM)
        .astype(jnp.bfloat16)
    )
    partial_value = jnp.dot(attended, w_out, preferred_element_type=jnp.float32)
    share = width // ten_count
    column = ten_rank * share
    attn_sum = lax.psum(partial_value.astype(jnp.bfloat16), "tensor").astype(jnp.float32)
    residual = (tokens.astype(jnp.float32) + attn_sum).astype(jnp.bfloat16)
    payload = rms_norm(residual, gain_moe)
    logits = jnp.dot(payload.astype(jnp.float32), w_router, preferred_element_type=jnp.float32)
    residual_share = lax.dynamic_slice_in_dim(residual, column, share, 1)
    topk = routes.shape[1]
    expert_ids = jnp.arange(EXPERTS, dtype=jnp.int32)
    picked = routes[:, :, None] == expert_ids[None, None, :]
    chosen = jnp.sum(jnp.where(picked, logits[:, None, :], 0.0), axis=2)
    gates = jax.nn.softmax(chosen, axis=1)
    capacity = rows // 2
    holders = seq_count // EXPERTS
    hits = jnp.any(picked, axis=1)
    row_index = jnp.arange(rows, dtype=jnp.int32)
    earlier = (row_index[None, :] < row_index[:, None]).astype(jnp.bfloat16)
    before = jnp.dot(
        earlier, hits.astype(jnp.bfloat16), preferred_element_type=jnp.float32
    ).astype(jnp.int32)
    slot_of = jnp.where(hits, before, -1)
    slot_index = jnp.arange(capacity, dtype=jnp.int32)
    sources = (slot_of.T[:, None, :] == slot_index[None, :, None]).astype(jnp.bfloat16)
    outgoing = (
        jnp.dot(
            sources.reshape(EXPERTS * capacity, rows), payload, preferred_element_type=jnp.float32
        )
        .astype(jnp.bfloat16)
        .reshape(EXPERTS, 1, capacity, payload.shape[1])
    )
    outgoing = jnp.broadcast_to(outgoing, (EXPERTS, holders, capacity, payload.shape[1])).reshape(
        seq_count, capacity, payload.shape[1]
    )
    received = lax.all_to_all(outgoing, "seq", split_axis=0, concat_axis=0, tiled=True)
    senders, count, columns = received.shape
    flat = received.reshape(senders * count, columns)
    gate_h = jnp.dot(flat, w_gate, preferred_element_type=jnp.float32)
    up_h = jnp.dot(flat, w_up, preferred_element_type=jnp.float32)
    active = (jax.nn.silu(gate_h) * up_h).astype(jnp.bfloat16)
    block_rows = jnp.dot(active, w_down, preferred_element_type=jnp.float32)
    summed = lax.psum_scatter(
        block_rows.astype(jnp.bfloat16), "tensor", scatter_dimension=1, tiled=True
    )
    returned = lax.all_to_all(
        summed.reshape(senders, count, summed.shape[1]),
        "seq",
        split_axis=0,
        concat_axis=0,
        tiled=True,
    )
    rank_of = jnp.sum(jnp.where(picked, before[:, None, :], 0), axis=2)
    place_of = routes * capacity + rank_of
    slots = jnp.arange(EXPERTS * capacity, dtype=jnp.int32)
    takes = (place_of.T[:, :, None] == slots[None, None, :]).astype(jnp.bfloat16)
    takes = jnp.broadcast_to(
        takes.reshape(topk, rows, EXPERTS, 1, capacity),
        (topk, rows, EXPERTS, holders, capacity),
    ).reshape(topk * rows, seq_count * capacity)
    per_route = jnp.dot(
        takes,
        returned.reshape(seq_count * capacity, share),
        preferred_element_type=jnp.float32,
    ).reshape(topk, rows, share)
    mixture = jnp.sum(gates.T[:, :, None] * per_route, axis=0)
    layer_out = (residual_share.astype(jnp.float32) + mixture).astype(jnp.bfloat16)
    return (layer_out, kv_cache)


def solution(mesh):
    return jax.shard_map(
        local,
        mesh=mesh,
        in_specs=(
            P("seq", None),
            P(),
            P("seq", None),
            P(),
            P(),
            P(None, "tensor"),
            P(None, "tensor"),
            P("tensor", None),
            P(),
            P(),
            P(None, ("seq", "tensor")),
            P(None, ("seq", "tensor")),
            P(("seq", "tensor"), None),
        ),
        out_specs=(P("seq", "tensor"), P("seq", "tensor")),
        check_vma=False,
    )
```

```python
import functools

import jax
import jax.numpy as jnp
from jax import lax
from jax.experimental import pallas as pl
from jax.experimental.pallas import tpu as pltpu
from jax.sharding import PartitionSpec as P

HEADS = 32
KV_HEADS = 8
HEAD_DIM = 128
EXPERTS = 8


EPS = 1e-05
THETA = 1000000.0
FLOOR = -1e30


def rms_norm(rows, gain):
    values = rows.astype(jnp.float32)
    scale = lax.rsqrt(jnp.mean(values * values, axis=-1, keepdims=True) + EPS)
    return (values * scale * gain).astype(jnp.bfloat16)


def rotate(values, position):
    half = values.shape[-1] // 2
    freqs = THETA ** (-(jnp.arange(half, dtype=jnp.float32) * 2.0) / values.shape[-1])
    angles = position.astype(jnp.float32)[:, None] * freqs[None, :]
    cosine = jnp.cos(angles)[:, None, :]
    sine = jnp.sin(angles)[:, None, :]
    first = values[..., :half]
    second = values[..., half:]
    return jnp.concatenate(
        [first * cosine - second * sine, second * cosine + first * sine], axis=-1
    )


def segment_layout(segment_ids, owners, token_index):
    short_count = owners.shape[0] - 1
    labels = jnp.where(segment_ids < 0, short_count + 1, segment_ids)
    mine = jnp.sum(
        jnp.where(
            jnp.arange(segment_ids.shape[0], dtype=jnp.int32)[None, :] == token_index[:, None],
            labels[None, :],
            0,
        ),
        axis=1,
    )
    seg_start = jnp.sum((labels[None, :] < mine[:, None]).astype(jnp.int32), axis=1)
    owner_ext = jnp.concatenate([owners, jnp.full((1,), -1, jnp.int32)])
    onehot = labels[:, None] == jnp.arange(short_count + 2, dtype=jnp.int32)[None, :]
    owner_all = jnp.sum(jnp.where(onehot, owner_ext[None, :], 0), axis=1)
    return (seg_start, owner_all)


def cache_places(owner_all, owner):
    total = owner_all.shape[0]
    index = jnp.arange(total, dtype=jnp.int32)
    mine = owner_all == owner
    slots = jnp.sum(((index[None, :] < index[:, None]) & mine[None, :]).astype(jnp.int32), axis=1)
    slots = jnp.where(mine, slots, total)
    return (index[:, None] == slots[None, :]).astype(jnp.bfloat16)


CHUNK = 1024
TILE = 256
SLOTS = 4


def expert_kernel(
    peers, capacity, holders, out_ref, wg_ref, wu_ref, wd_ref, ret_ref,
    recv, gu, wd, acc_g, acc_u, active, y,
    gu_sem, wd_sem, own_sem, ret_own_sem, send_sem, recv_sem, back_send_sem, back_recv_sem,
):
    me = lax.axis_index("seq")
    ten = lax.axis_index("tensor")
    width = out_ref.shape[1]
    hidden = wg_ref.shape[1]
    chunks = width // CHUNK
    tiles = hidden // TILE

    def rows_of(index):
        return pl.ds(pl.multiple_of(index * capacity, capacity), capacity)

    def columns_of(chunk):
        return pl.ds(chunk * CHUNK, CHUNK)

    def peer(step):
        return lax.rem(me + step, peers)

    def load_gu(number):
        source = wg_ref if number % 2 == 0 else wu_ref
        return pltpu.make_async_copy(
            source.at[columns_of(number // 2), :], gu.at[number % SLOTS], gu_sem.at[number % SLOTS]
        )

    def load_wd(chunk):
        return pltpu.make_async_copy(wd_ref.at[:, columns_of(chunk)], wd.at[chunk], wd_sem.at[chunk])

    def send(chunk, step):
        return pltpu.make_async_remote_copy(
            src_ref=out_ref.at[rows_of(peer(step) // holders), columns_of(chunk)],
            dst_ref=recv.at[rows_of(me), columns_of(chunk)],
            send_sem=send_sem.at[chunk, step],
            recv_sem=recv_sem.at[chunk, step],
            device_id=(peer(step), ten),
            device_id_type=pl.DeviceIdType.MESH,
        )

    def give_back(chunk, step):
        return pltpu.make_async_remote_copy(
            src_ref=y.at[rows_of(peer(step)), columns_of(chunk)],
            dst_ref=ret_ref.at[rows_of(me), columns_of(chunk)],
            send_sem=back_send_sem.at[chunk, step],
            recv_sem=back_recv_sem.at[chunk, step],
            device_id=(peer(step), ten),
            device_id_type=pl.DeviceIdType.MESH,
        )

    def keep(chunk):
        return pltpu.make_async_copy(
            y.at[rows_of(me), columns_of(chunk)],
            ret_ref.at[rows_of(me), columns_of(chunk)],
            ret_own_sem.at[chunk],
        )

    own = pltpu.make_async_copy(out_ref.at[rows_of(me // holders), :], recv.at[rows_of(me), :], own_sem)
    for number in range(SLOTS):
        load_gu(number).start()
    own.start()
    barrier = pltpu.get_barrier_semaphore()
    for step in range(1, peers):
        pl.semaphore_signal(
            barrier, inc=1, device_id=(peer(step), ten), device_id_type=pl.DeviceIdType.MESH
        )
    pl.semaphore_wait(barrier, peers - 1)
    for chunk in range(chunks):
        for step in range(1, peers):
            send(chunk, step).start()
    for chunk in range(chunks):
        load_wd(chunk).start()
    own.wait()
    for chunk in range(chunks):
        for step in range(1, peers):
            send(chunk, step).wait_recv()
        for part, acc in ((0, acc_g), (1, acc_u)):
            number = 2 * chunk + part
            load_gu(number).wait()

            @pl.loop(0, tiles)
            def _(tile):
                columns = pl.ds(pl.multiple_of(tile * TILE, TILE), TILE)
                product = jnp.dot(
                    recv[:, columns_of(chunk)],
                    gu[number % SLOTS, :, columns],
                    preferred_element_type=jnp.float32,
                )
                if chunk == 0:
                    acc[:, columns] = product
                else:
                    acc[:, columns] += product

            if number + SLOTS < 2 * chunks:
                load_gu(number + SLOTS).start()

    @pl.loop(0, tiles)
    def _(tile):
        columns = pl.ds(pl.multiple_of(tile * TILE, TILE), TILE)
        gate = acc_g[:, columns]
        active[:, columns] = (gate / (1.0 + jnp.exp(-gate)) * acc_u[:, columns]).astype(jnp.bfloat16)

    for chunk in range(chunks):
        load_wd(chunk).wait()

        @pl.loop(0, CHUNK // TILE)
        def _(tile):
            start = pl.multiple_of(tile * TILE, TILE)
            y[:, pl.ds(pl.multiple_of(chunk * CHUNK + start, TILE), TILE)] = jnp.dot(
                active[...], wd[chunk, :, pl.ds(start, TILE)], preferred_element_type=jnp.float32
            ).astype(jnp.bfloat16)

        for step in range(1, peers):
            give_back(chunk, step).start()
        keep(chunk).start()
    for chunk in range(chunks):
        keep(chunk).wait()
        for step in range(1, peers):
            send(chunk, step).wait_send()
            give_back(chunk, step).wait_send()
            give_back(chunk, step).wait_recv()


def experts(outgoing, w_gate, w_up, w_down, peers, capacity, holders):
    width = outgoing.shape[1]
    hidden = w_gate.shape[1]
    count = peers * capacity
    chunks = width // CHUNK
    dma = pltpu.SemaphoreType.DMA
    return pl.pallas_call(
        functools.partial(expert_kernel, peers, capacity, holders),
        out_shape=jax.ShapeDtypeStruct((count, width), jnp.bfloat16),
        in_specs=[pl.BlockSpec(memory_space=pl.ANY)] * 4,
        out_specs=pl.BlockSpec(memory_space=pl.ANY),
        scratch_shapes=[
            pltpu.VMEM((count, width), jnp.bfloat16),
            pltpu.VMEM((SLOTS, CHUNK, hidden), jnp.bfloat16),
            pltpu.VMEM((chunks, hidden, CHUNK), jnp.bfloat16),
            pltpu.VMEM((count, hidden), jnp.float32),
            pltpu.VMEM((count, hidden), jnp.float32),
            pltpu.VMEM((count, hidden), jnp.bfloat16),
            pltpu.VMEM((count, width), jnp.bfloat16),
            dma((SLOTS,)),
            dma((chunks,)),
            dma,
            dma((chunks,)),
            dma((chunks, peers)),
            dma((chunks, peers)),
            dma((chunks, peers)),
            dma((chunks, peers)),
        ],
        compiler_params=pltpu.CompilerParams(
            collective_id=0, has_side_effects=True, vmem_limit_bytes=58 * 2**20
        ),
        cost_estimate=pl.CostEstimate(
            flops=6 * count * width * hidden,
            bytes_accessed=6 * width * hidden + 4 * count * width,
            transcendentals=count * hidden,
        ),
    )(outgoing, w_gate, w_up, w_down)


def local(
    tokens,
    segment_ids,
    routes,
    owners,
    gain_attn,
    w_query,
    w_kv,
    w_out,
    gain_moe,
    w_router,
    w_gate,
    w_up,
    w_down,
):
    seq_count = lax.axis_size("seq")
    ten_count = lax.axis_size("tensor")
    seq_rank = lax.axis_index("seq")
    ten_rank = lax.axis_index("tensor")
    rows, width = tokens.shape
    kv_local = w_kv.shape[1] // (2 * HEAD_DIM)
    kv_width = 2 * kv_local * HEAD_DIM
    group = HEADS // KV_HEADS
    first = seq_rank * rows
    token_index = first + jnp.arange(rows, dtype=jnp.int32)
    seg_start, owner_all = segment_layout(segment_ids, owners, token_index)
    position = token_index - seg_start
    normed = rms_norm(tokens, gain_attn)
    queries = jnp.dot(normed, w_query, preferred_element_type=jnp.float32).reshape(
        rows, kv_local * group, HEAD_DIM
    )
    queries = rotate(queries, position).astype(jnp.bfloat16)
    pairs = jnp.dot(normed, w_kv, preferred_element_type=jnp.float32).reshape(
        rows, kv_local, 2, HEAD_DIM
    )
    keys = rotate(pairs[:, :, 0], position).astype(jnp.bfloat16)
    values = pairs[:, :, 1].astype(jnp.bfloat16)
    grouped = queries.reshape(rows, kv_local, group, HEAD_DIM)
    scale = HEAD_DIM ** (-0.5)
    kv_rows = jnp.stack([keys, values], axis=2).reshape(rows, kv_width)
    piece = lax.all_gather(kv_rows, "seq", axis=0, tiled=True)
    kv_cache = jnp.dot(
        cache_places(owner_all, seq_rank), piece, preferred_element_type=jnp.float32
    ).astype(jnp.bfloat16)
    running = jnp.full((kv_local, group, rows), FLOOR, jnp.float32)
    count = piece.shape[0]
    pieces = piece.reshape(count, kv_local, 2, HEAD_DIM)
    key_piece = pieces[:, :, 0]
    value_piece = pieces[:, :, 1]
    key_index = jnp.arange(count, dtype=jnp.int32)
    allowed = (key_index[None, :] <= token_index[:, None]) & (
        key_index[None, :] >= seg_start[:, None]
    )
    scores = (
        jnp.einsum("qkgd,nkd->kgqn", grouped, key_piece, preferred_element_type=jnp.float32) * scale
    )
    scores = jnp.where(allowed[None, None], scores, FLOOR)
    new_top = jnp.maximum(running, jnp.max(scores, axis=-1))
    weights = jnp.where(allowed[None, None], jnp.exp(scores - new_top[..., None]), 0.0)
    mass = jnp.sum(weights, axis=-1)
    accum = jnp.einsum(
        "kgqn,nkd->kgqd",
        weights.astype(jnp.bfloat16),
        value_piece,
        preferred_element_type=jnp.float32,
    )
    running, mass, accum = (new_top, mass, accum)
    attended = (
        (accum / mass[..., None])
        .transpose(2, 0, 1, 3)
        .reshape(rows, kv_local * group * HEAD_DIM)
        .astype(jnp.bfloat16)
    )
    partial_value = jnp.dot(attended, w_out, preferred_element_type=jnp.float32)
    share = width // ten_count
    column = ten_rank * share
    attn_sum = lax.psum(partial_value.astype(jnp.bfloat16), "tensor").astype(jnp.float32)
    residual = (tokens.astype(jnp.float32) + attn_sum).astype(jnp.bfloat16)
    payload = rms_norm(residual, gain_moe)
    logits = jnp.dot(payload.astype(jnp.float32), w_router, preferred_element_type=jnp.float32)
    residual_share = lax.dynamic_slice_in_dim(residual, column, share, 1)
    topk = routes.shape[1]
    expert_ids = jnp.arange(EXPERTS, dtype=jnp.int32)
    picked = routes[:, :, None] == expert_ids[None, None, :]
    chosen = jnp.sum(jnp.where(picked, logits[:, None, :], 0.0), axis=2)
    gates = jax.nn.softmax(chosen, axis=1)
    capacity = rows // 2
    holders = seq_count // EXPERTS
    hits = jnp.any(picked, axis=1)
    row_index = jnp.arange(rows, dtype=jnp.int32)
    earlier = (row_index[None, :] < row_index[:, None]).astype(jnp.bfloat16)
    before = jnp.dot(
        earlier, hits.astype(jnp.bfloat16), preferred_element_type=jnp.float32
    ).astype(jnp.int32)
    slot_of = jnp.where(hits, before, -1)
    slot_index = jnp.arange(capacity, dtype=jnp.int32)
    sources = (slot_of.T[:, None, :] == slot_index[None, :, None]).astype(jnp.bfloat16)
    outgoing = (
        jnp.dot(
            sources.reshape(EXPERTS * capacity, rows), payload, preferred_element_type=jnp.float32
        )
        .astype(jnp.bfloat16)
    )
    returned = experts(outgoing, w_gate, w_up, w_down, seq_count, capacity, holders)
    rank_of = jnp.sum(jnp.where(picked, before[:, None, :], 0), axis=2)
    place_of = routes * capacity + rank_of
    slots = jnp.arange(EXPERTS * capacity, dtype=jnp.int32)
    takes = (place_of.T[:, :, None] == slots[None, None, :]).astype(jnp.bfloat16)
    takes = jnp.broadcast_to(
        takes.reshape(topk, rows, EXPERTS, 1, capacity),
        (topk, rows, EXPERTS, holders, capacity),
    ).reshape(topk * rows, seq_count * capacity)
    per_route = jnp.dot(takes, returned, preferred_element_type=jnp.float32).reshape(
        topk, rows, width
    )
    mixture_part = jnp.sum(gates.T[:, :, None] * per_route, axis=0).astype(jnp.bfloat16)
    mixture = lax.psum_scatter(mixture_part, "tensor", scatter_dimension=1, tiled=True)
    layer_out = (residual_share.astype(jnp.float32) + mixture.astype(jnp.float32)).astype(
        jnp.bfloat16
    )
    return (layer_out, kv_cache)


def solution(mesh):
    return jax.shard_map(
        local,
        mesh=mesh,
        in_specs=(
            P("seq", None),
            P(),
            P("seq", None),
            P(),
            P(),
            P(None, "tensor"),
            P(None, "tensor"),
            P("tensor", None),
            P(),
            P(),
            P(None, ("seq", "tensor")),
            P(None, ("seq", "tensor")),
            P(("seq", "tensor"), None),
        ),
        out_specs=(P("seq", "tensor"), P("seq", "tensor")),
        check_vma=False,
    )
```
